1024 devices in a mesh: row: 8 (over y, x_lo), col: 128 (over x_hi, z, core).
Axes of the slice: x: 4 (x_hi: 2, x_lo: 2; x = x_hi * 2 + x_lo), y: 4, z: 32, core: 2. Of those that a mesh axis runs over, the one named last changes fastest.
Arguments:
- inputs: bfloat16 [1536, 1024], P(None, 'row'), may hold values from -6 to 6
- out_grad: bfloat16 [1536, 1024], P(None, 'row'), may hold values from -1.5 to 1.5
- w_in: bfloat16 [1024, 65536], P('row', 'col'), may hold values from -0.25 to 0.25
- w_out: bfloat16 [65536, 1024], P('col', 'row'), may hold values from -0.1875 to 0.1875
- in_keep: int32 [8, 512], P('row', 'col'), may hold values from 0 to 1, as said below
- out_keep: int32 [512, 8], P('col', 'row'), may hold values from 0 to 1, as said below
Outputs:
- w_in_grad: float32 [1024, 65536], P('row', 'col')
- w_out_grad: float32 [65536, 1024], P('col', 'row')
- in_grad: float32 [1536, 1024], P('col', 'row')
The draws below stay inside these ranges and needn't reach their ends.
Inputs may be any that keep to these rules, and one draw needn't show every extreme that they name: `in_keep`: 1 where the 128 x 128 block of w_in is kept, 0 where it is pruned. `out_keep`: 1 where the 128 x 128 block of w_out is kept, 0 where it is pruned.
All inputs are finite; a program needn't handle non-finite values.
Results may differ from the reference program's by a relative error of at most 0.018.
Values may be sent and summed in bfloat16 or wider, within the bound.
A program may use at most 32 MiB of HBM per device.

```python
import jax
import jax.numpy as jnp
from jax import lax

D = 1024
FF = 65536
BLOCK = 128
TOKENS = 1536
N_ROW = 8


def draw_in_keep(key, part):
    key = jax.random.fold_in(key, 11)
    level_key, roll_key = jax.random.split(key)
    levels = jax.random.randint(level_key, (1, FF // BLOCK), 1, 8)
    rolls = jax.random.randint(roll_key, (D // BLOCK, FF // BLOCK), 0, 8)
    return (rolls < levels).astype(jnp.int32)


def draw_out_keep(key, part):
    key = jax.random.fold_in(key, 23)
    level_key, roll_key = jax.random.split(key)
    levels = jax.random.randint(level_key, (FF // BLOCK, 1), 1, 8)
    rolls = jax.random.randint(roll_key, (FF // BLOCK, D // BLOCK), 0, 8)
    return (rolls < levels).astype(jnp.int32)


def steps_of(rng, extent, cuts, low, top_value):
    loudness, own = 1.0, jax.random.fold_in(rng, 6)
    for position, blocks in cuts:
        heights = jnp.exp(jax.random.uniform(jax.random.fold_in(own, position), (blocks,), jnp.float32, low / len(cuts), top_value / len(cuts)))
        loudness = loudness * jnp.repeat(heights, extent[position] // blocks).reshape([-1 if axis == position else 1 for axis in range(len(extent))])
    return loudness


def scatter_about(key, dims, deviation, reach, cuts=(), kind=jnp.bfloat16):
    values = deviation * jax.random.normal(key, dims, jnp.float32)
    if cuts:
        values = values * steps_of(key, dims, cuts, -0.22, 0.18)
    return jnp.clip(values, -reach, reach).astype(kind)


def setup_inputs(seed: int = 0) -> dict:
    streams_of = jax.random.split(jax.random.key(seed), 7)
    return {
        "inputs": scatter_about(streams_of[0], (TOKENS, D), 1.0, 6.0, ((1, 8),)),
        "out_grad": scatter_about(streams_of[1], (TOKENS, D), 0.25, 1.5, ((1, 8),)),
        "w_in": scatter_about(streams_of[2], (D, FF), (D // 2) ** -0.5, 0.25, ((0, 8), (1, 128))),
        "w_out": scatter_about(streams_of[3], (FF, D), D ** -0.5, 0.1875, ((0, 128), (1, 8))),
        "in_keep": draw_in_keep(jax.random.fold_in(streams_of[6], 71), 0),
        "out_keep": draw_out_keep(jax.random.fold_in(streams_of[6], 71), 0),
    }


sqrt_two_pi = 0.7978845608028654
cubic_term = 0.044715

def prune_blocks(weight, keep):
    rows, cols = weight.shape
    blocks = weight.reshape(rows // BLOCK, BLOCK, cols // BLOCK, BLOCK)
    kept = jnp.where(keep[:, None, :, None] > 0, blocks, jnp.zeros_like(blocks))
    return kept.reshape(rows, cols)

def gelu_parts(value):
    tangent = jnp.tanh(sqrt_two_pi * (value + cubic_term * value * value * value))
    activated = 0.5 * value * (1.0 + tangent)
    gradient = 0.5 * (1.0 + tangent) + 0.5 * value * (1.0 - tangent * tangent) * sqrt_two_pi * (1.0 + 3.0 * cubic_term * value * value)
    return (activated, gradient)

def rounded(term):
    return lax.optimization_barrier(term.astype(jnp.bfloat16)).astype(jnp.float32)

def reference(inputs, out_grad, w_in, w_out, in_keep, out_keep):
    kept_in = prune_blocks(w_in, in_keep)
    kept_out = prune_blocks(w_out, out_keep)
    width = D // N_ROW
    pre_act = jnp.zeros((TOKENS, FF), jnp.float32)
    act_grad = jnp.zeros((TOKENS, FF), jnp.float32)
    for member in range(N_ROW):
        first = member * width
        left = inputs[:, first:first + width]
        term = jnp.dot(left, kept_in[first:first + width, :], preferred_element_type=jnp.float32)
        pre_act = pre_act + rounded(term)
        cot_left = out_grad[:, first:first + width]
        back_term = lax.dot_general(cot_left, kept_out[:, first:first + width], (((1,), (1,)), ((), ())), preferred_element_type=jnp.float32)
        act_grad = act_grad + rounded(back_term)
    activated, gradient = gelu_parts(pre_act)
    activated = activated.astype(jnp.bfloat16)
    pre_grad = (act_grad * gradient).astype(jnp.bfloat16)
    w_in_grad = lax.dot_general(inputs, pre_grad, (((0,), (0,)), ((), ())), preferred_element_type=jnp.float32)
    w_out_grad = lax.dot_general(activated, out_grad, (((0,), (0,)), ((), ())), preferred_element_type=jnp.float32)
    in_grad = lax.dot_general(pre_grad, kept_in, (((1,), (1,)), ((), ())), preferred_element_type=jnp.float32)
    return (prune_blocks(w_in_grad, in_keep), prune_blocks(w_out_grad, out_keep), in_grad)
```

```python
import jax
import jax.numpy as jnp
from jax import lax
from jax.experimental import pallas as pl
from jax.experimental.pallas import tpu as pltpu
from jax.sharding import PartitionSpec as P

MESH = pl.DeviceIdType.MESH
BLOCK = 128
BF = jnp.bfloat16
F32 = jnp.float32

sqrt_two_pi = 0.7978845608028654
cubic_term = 0.044715

N_Y, N_XL, N_XH, N_Z = 4, 2, 2, 32
TOK = 384
HALF = 192
HID = 256
ROWS = 12


def gelu_parts(value):
    square = value * value
    tangent = jnp.tanh(sqrt_two_pi * value * (1.0 + cubic_term * square))
    upper = 0.5 * (1.0 + tangent)
    gradient = upper + 0.5 * value * (1.0 - tangent * tangent) * sqrt_two_pi * (
        1.0 + 3.0 * cubic_term * square
    )
    return value * upper, gradient


def nn(a, b):
    return jnp.dot(a, b, preferred_element_type=F32)


def nt(a, b):
    return lax.dot_general(a, b, (((1,), (1,)), ((), ())), preferred_element_type=F32)


class Names:
    def __init__(self):
        self.of = {}

    def __call__(self, *name):
        return self.of.setdefault(name, len(self.of))


N_SEM = 96


def kernel(
    inputs, out_grad, w_in, w_out, in_keep, out_keep,
    o_in, o_out, o_x,
    acts, win, wout, win_l, wout_l, win_s, wout_s, kin, kout, acts_t, pre, ag,
    v_in, v_out, ya_in, yb_out, y1_in, y1_out, y3_in, y3_out, s_in, s_out, x_in, x_out,
    q_b, q_r, q_s, z_r, f_s, f_r,
    send_sem, recv_sem, local_sem, relay_sem,
):
    row, col = lax.axis_index("row"), lax.axis_index("col")
    y, xl = row // N_XL, row % N_XL
    xh, z, k = col // (2 * N_Z), (col // 2) % N_Z, col % 2
    x = 2 * xh + xl
    h = z % 2
    pair = z + 1 - 2 * h

    def dev(y=y, x=x, z=z, k=k):
        return (y * N_XL + x % 2, ((x // 2) * N_Z + z) * 2 + k)

    def up(d):
        return (y + d) % N_Y

    def xr(d):
        return (x + d) % 4

    def along_z(d):
        return dev(z=(z + d + N_Z) % N_Z)

    core = dev(k=1 - k)
    inner = dev(x=2 * xh + 1 - xl)
    ydev = {d: dev(y=up(d)) for d in (1, 2, 3)}
    xdev = {d: dev(x=xr(d)) for d in (1, 3)}
    near = {
        (e, f): dev(x=xr(e), z=pair if f else z) for f in (0, 1) for e in range(4) if e or f
    }

    def owner(j):
        return dev(
            y=2 * (1 - xh) + k, x=2 * (y // 2) + xl, z=16 * (y % 2) + 8 * h + j // 2, k=j % 2
        )

    barrier = pltpu.get_barrier_semaphore()
    partners = [core, *ydev.values(), *near.values(), along_z(2 * h - 1)]
    partners += [dev(y=2 * xh + i, x=2 * (1 - y // 2) + xl, k=y % 2) for i in (0, 1)]
    for device in partners:
        pl.semaphore_signal(barrier, inc=1, device_id=device, device_id_type=MESH)

    names = Names()
    sent = []

    def copy(src, dst, name, device):
        i = names(*name)
        return pltpu.make_async_remote_copy(
            src_ref=src, dst_ref=dst, send_sem=send_sem.at[i], recv_sem=recv_sem.at[i],
            device_id=device, device_id_type=MESH,
        )

    def send(src, dst, name, device):
        c = copy(src, dst, name, device)
        c.start()
        sent.append(c)

    def arrived(dst, name):
        copy(dst, dst, name, core).wait_recv()

    def tell(r):
        for d in (-(1, 1, 2, 4, 8)[r], (1, 1, 2, 4, 8)[r]):
            pl.semaphore_signal(
                relay_sem.at[r], inc=1, device_id=along_z(d), device_id_type=MESH
            )

    def heard(r):
        pl.semaphore_wait(relay_sem.at[r], 2)

    local = [
        pltpu.make_async_copy(src, dst, local_sem.at[i])
        for i, (src, dst) in enumerate(
            ((w_in, win_l), (w_out, wout_l), (in_keep, kin), (out_keep, kout))
        )
    ]
    for c in local:
        c.start()
    for c in local:
        c.wait()

    def pruned_in(j):
        at = pl.ds(pl.multiple_of(j * BLOCK, BLOCK), BLOCK)
        return (win_l[:, at].astype(F32) * kin[0, j].astype(F32)).astype(BF)

    def pruned_out(j):
        at = pl.ds(pl.multiple_of(j * BLOCK, BLOCK), BLOCK)
        return (wout_l[at, :].astype(F32) * kout[0, j].astype(F32)).astype(BF)

    for jj in range(2):
        part = pl.ds(BLOCK * jj, BLOCK)
        win_s[:, part] = pruned_in(2 * (1 - xl) + jj)
        wout_s[part, :] = pruned_out(2 * (1 - xl) + jj)
        win[0, 0:BLOCK, part] = pruned_in(2 * xl + jj)
        wout[0, part, 0:BLOCK] = pruned_out(2 * xl + jj)

    pl.semaphore_wait(barrier, len(partners))

    mine = pl.ds(pl.multiple_of(HALF * xh, HALF), HALF)
    other = pl.ds(pl.multiple_of(HALF * (1 - xh), HALF), HALF)

    def tokens(of_y):
        return pl.ds(pl.multiple_of(TOK * of_y + HALF * xh, HALF), HALF)

    lo, hi = pl.ds(0, BLOCK), pl.ds(BLOCK, BLOCK)

    def win_at(d, p):
        return win.at[d, pl.ds(BLOCK * p, BLOCK), :]

    def wout_at(d, p):
        return wout.at[d, :, pl.ds(BLOCK * p, BLOCK)]

    def own_tokens(array):
        at = pl.ds(pl.multiple_of(TOK * y, TOK), TOK)
        return pltpu.make_async_copy(array.at[at, :], acts.at[k, 0, :, lo], local_sem.at[4])

    def first_copies(array):
        along_y = [
            copy(array.at[tokens(up(d)), :], acts.at[k, 4 - d, mine, lo], ("ay", 4 - d), ydev[d])
            for d in (1, 3, 2)
        ]
        along_x = [
            copy(array.at[tokens(y), :], acts.at[k, 0, mine, hi], ("ax", 0, 4 - d), xdev[d])
            for d in (1, 3)
        ]
        return along_y + along_x

    send(win_s, win_at(0, 1), ("wx_in",), inner)
    send(wout_s, wout_at(0, 1), ("wx_out",), inner)

    for i, array in enumerate((inputs, out_grad)):

        @pl.when(k == i)
        def _():
            for c in first_copies(array):
                c.start()
            own_tokens(array).start()

    sent += first_copies(inputs)

    def spread(p):
        for d in (1, 3):
            send(win_at(0, p), win_at(4 - d, p), ("wy_in", 4 - d, p), ydev[d])
            send(wout_at(0, p), wout_at(4 - d, p), ("wy_out", 4 - d, p), ydev[d])

    spread(0)
    tell(0)

    def pass_on(p):
        arrived(win_at(3, p), ("wy_in", 3, p))
        send(win_at(3, p), win_at(2, p), ("wf_in", p), ydev[1])
        arrived(wout_at(1, p), ("wy_out", 1, p))
        send(wout_at(1, p), wout_at(2, p), ("wf_out", p), ydev[3])

    def token_half(e):
        return pl.ds(pl.multiple_of(HALF * (xr(e) // 2), HALF), HALF)

    def from_x(d, e):
        return acts.at[k, d, token_half(e), hi]

    def both_x(d):
        for e in (1, 3):
            arrived(from_x(d, e), ("ax", d, e))
        if d == 2:
            away = 1 + 2 * k
            half = pl.ds(pl.multiple_of(HALF * (((x + 4 - away) % 4) // 2), HALF), HALF)
            send(
                acts.at[k, d, half, hi], acts.at[k, d, half, lo], ("af", d), dev(x=(x + away) % 4)
            )
        elif d:
            send(from_x(d, d), acts.at[k, d, token_half(d), lo], ("af", d), xdev[4 - d])

    def to_core(d):
        if d:
            arrived(acts.at[k, d, other, lo], ("af", d))
        send(acts.at[k, d], acts.at[k, d], ("ac", d), core)

    def products(d):
        for p in (0, 1):
            if d == 1:
                arrived(win_at(1, p), ("wy_in", 1, p))
            if d == 3:
                arrived(wout_at(3, p), ("wy_out", 3, p))
            if d == 2:
                arrived(win_at(2, p), ("wf_in", p))
                arrived(wout_at(2, p), ("wf_out", p))
        arrived(acts.at[1 - k, d], ("ac", d))
        a, b = nn(acts[0, d], win[d]), nt(acts[1, d], wout[d])
        if d == 0:
            pre[...], ag[...] = a, b
        else:
            pre[...] += a
            ag[...] += b

    for d in (3, 1, 2):
        here = acts.at[k, d, mine, lo]
        arrived(here, ("ay", d))
        for e in (1, 3):
            send(here, acts.at[k, d, mine, hi], ("ax", d, 4 - e), xdev[e])
        if d == 3:
            heard(0)
            tell(1)

    arrived(win_at(0, 1), ("wx_in",))
    arrived(wout_at(0, 1), ("wx_out",))
    spread(1)
    heard(1)
    tell(2)
    pass_on(0)
    own_tokens(inputs).wait()
    both_x(0)
    to_core(0)
    both_x(3)
    heard(2)
    tell(3)
    both_x(1)
    pass_on(1)
    both_x(2)
    to_core(3)
    products(0)
    to_core(1)
    products(3)
    to_core(2)
    heard(3)
    tell(4)
    products(1)
    products(2)

    activated, gradient = gelu_parts(pre[...])
    pg = (ag[...] * gradient).astype(BF)
    act_t = activated.astype(BF).T

    def slices(s, i):
        of_y = s + 2 * i
        q = nt(pg, win[(of_y - y + N_Y) % N_Y]).astype(BF)
        q_b[s, 2 * (1 - i) + xl] = q[:, 0:BLOCK]
        q_b[s, 2 * (1 - i) + 1 - xl] = q[:, BLOCK:]

    for i in (0, 1):
        slices(1 - k, i)
        half = pl.ds(2 * (1 - i), 2)
        send(q_b.at[1 - k, half], q_r.at[half], ("q", i), core)
    for i in (0, 1):
        slices(k, i)

    def rows_of(f):
        return pl.ds(pl.multiple_of(HALF * ((h + f) % 2), HALF), HALF)

    for i in (0, 1):
        half = pl.ds(2 * (1 - i), 2)
        arrived(q_r.at[half], ("q", i))
        q_s[half] = (q_b[k, half].astype(F32) + q_r[half].astype(F32)).astype(BF)

    for e, f in ((2, 1), (1, 1), (3, 1), (2, 0), (1, 0), (3, 0), (0, 1)):
        send(
            q_s.at[xr(e), rows_of(f)], z_r.at[4 * f + (4 - e) % 4], ("z", (4 - e) % 4, f), near[e, f]
        )
    total = q_s[x, rows_of(0)].astype(F32)
    for e, f in ((1, 0), (3, 0), (0, 1), (1, 1), (3, 1), (2, 0), (2, 1)):
        arrived(z_r.at[4 * f + e], ("z", e, f))
        total += z_r[4 * f + e].astype(F32)

    f_s[...] = jnp.zeros_like(f_s)
    for j in range(16):
        f_s[j, 0:ROWS] = total[ROWS * j : ROWS * (j + 1)].astype(BF)
    heard(4)
    group = z // 2
    first = [names("f", g) for g in range(16)][0]
    for j in range(16):
        c = pltpu.make_async_remote_copy(
            src_ref=f_s.at[j], dst_ref=f_r.at[group], send_sem=send_sem.at[first + j],
            recv_sem=recv_sem.at[first + group], device_id=owner(j), device_id_type=MESH,
        )
        c.start()
        sent.append(c)

    def grads(d):
        acts_t[...] = acts[0, d].T
        v_in[d] = nn(acts_t[...], pg).astype(BF)
        v_out[d] = nn(act_t, acts[1, d]).astype(BF)

    grads(2)
    send(v_in.at[2], ya_in, ("ya",), ydev[1])
    send(v_out.at[2], yb_out, ("yb",), ydev[3])
    grads(1)
    send(v_out.at[1], y1_out, ("y1_out",), ydev[1])
    grads(3)
    send(v_in.at[3], y3_in, ("y3_in",), ydev[3])
    grads(0)

    arrived(ya_in, ("ya",))
    v_in[1] = (v_in[1].astype(F32) + ya_in[...].astype(F32)).astype(BF)
    send(v_in.at[1], y1_in, ("y1_in",), ydev[1])
    arrived(yb_out, ("yb",))
    v_out[3] = (v_out[3].astype(F32) + yb_out[...].astype(F32)).astype(BF)
    send(v_out.at[3], y3_out, ("y3_out",), ydev[3])

    arrived(y1_in, ("y1_in",))
    arrived(y3_in, ("y3_in",))
    s_in[...] = v_in[0].astype(F32) + y1_in[...].astype(F32) + y3_in[...].astype(F32)
    x_in[0] = s_in[BLOCK:].astype(BF)
    send(x_in.at[0], x_in.at[1], ("gx_in",), inner)
    arrived(y1_out, ("y1_out",))
    arrived(y3_out, ("y3_out",))
    s_out[...] = v_out[0].astype(F32) + y1_out[...].astype(F32) + y3_out[...].astype(F32)
    x_out[0] = s_out[:, BLOCK:].astype(BF)
    send(x_out.at[0], x_out.at[1], ("gx_out",), inner)

    def store_in(j, value):
        at = pl.ds(pl.multiple_of(j * BLOCK, BLOCK), BLOCK)
        o_in[:, at] = value * kin[0, j].astype(F32)

    def store_out(j, value):
        at = pl.ds(pl.multiple_of(j * BLOCK, BLOCK), BLOCK)
        o_out[at, :] = value * kout[0, j].astype(F32)

    cuts = [pl.ds(BLOCK * jj, BLOCK) for jj in (0, 1)]
    for jj, cut in enumerate(cuts):
        store_in(2 * xl + jj, s_in[0:BLOCK, cut])
        store_out(2 * xl + jj, s_out[cut, 0:BLOCK])
    arrived(x_in.at[1], ("gx_in",))
    for jj, cut in enumerate(cuts):
        store_in(2 * (1 - xl) + jj, x_in[1, :, cut].astype(F32))
    arrived(x_out.at[1], ("gx_out",))
    for jj, cut in enumerate(cuts):
        store_out(2 * (1 - xl) + jj, x_out[1, cut, :].astype(F32))

    for c in sent:
        c.wait_send()

    for g in range(16):
        arrived(f_r.at[g], ("f", g))
    last = f_r[0].astype(F32)
    for g in range(1, 16):
        last += f_r[g].astype(F32)
    o_x[...] = last[0:ROWS]


def per_device(inputs, out_grad, w_in, w_out, in_keep, out_keep):
    arrays = [
        pltpu.with_memory_space_constraint(array, pltpu.HBM)
        for array in (inputs, out_grad, w_in, w_out, in_keep, out_keep.reshape(1, -1))
    ]
    vmem = pl.BlockSpec(memory_space=pltpu.VMEM)
    hbm = pl.BlockSpec(memory_space=pltpu.HBM)
    B, H, V = BLOCK, HID, pltpu.VMEM
    return pl.pallas_call(
        kernel,
        out_shape=(
            jax.ShapeDtypeStruct((B, 2 * H), F32),
            jax.ShapeDtypeStruct((2 * H, B), F32),
            jax.ShapeDtypeStruct((ROWS, B), F32),
        ),
        in_specs=[hbm] * 6,
        out_specs=[vmem, vmem, vmem],
        scratch_shapes=[
            V((2, 4, TOK, 2 * B), BF),
            V((4, 2 * B, H), BF),
            V((4, H, 2 * B), BF),
            V((B, 2 * H), BF),
            V((2 * H, B), BF),
            V((B, H), BF),
            V((H, B), BF),
            pltpu.SMEM((1, 4), jnp.int32),
            pltpu.SMEM((1, 4), jnp.int32),
            V((2 * B, TOK), BF),
            V((TOK, H), F32),
            V((TOK, H), F32),
            V((4, 2 * B, H), BF),
            V((4, H, 2 * B), BF),
            V((2 * B, H), BF),
            V((H, 2 * B), BF),
            V((2 * B, H), BF),
            V((H, 2 * B), BF),
            V((2 * B, H), BF),
            V((H, 2 * B), BF),
            V((2 * B, H), F32),
            V((H, 2 * B), F32),
            V((2, B, H), BF),
            V((2, H, B), BF),
            V((2, 4, TOK, B), BF),
            V((4, TOK, B), BF),
            V((4, TOK, B), BF),
            V((8, HALF, B), BF),
            V((16, 16, B), BF),
            V((16, 16, B), BF),
            pltpu.SemaphoreType.DMA((N_SEM,)),
            pltpu.SemaphoreType.DMA((N_SEM,)),
            pltpu.SemaphoreType.DMA((5,)),
            pltpu.SemaphoreType.REGULAR((5,)),
        ],
        compiler_params=pltpu.CompilerParams(
            collective_id=0, has_side_effects=True, vmem_limit_bytes=48 * 1024 * 1024
        ),
    )(*arrays)


def solution(mesh):
    return jax.shard_map(
        per_device,
        mesh=mesh,
        in_specs=(
            P(None, "row"),
            P(None, "row"),
            P("row", "col"),
            P("col", "row"),
            P("row", "col"),
            P("col", "row"),
        ),
        out_specs=(P("row", "col"), P("col", "row"), P("col", "row")),
        check_vma=False,
    )
```

```python
import jax
import jax.numpy as jnp
from jax import lax
from jax.experimental import pallas as pl
from jax.experimental.pallas import tpu as pltpu
from jax.sharding import PartitionSpec as P

MESH = pl.DeviceIdType.MESH
BLOCK = 128
BF = jnp.bfloat16
F32 = jnp.float32

sqrt_two_pi = 0.7978845608028654
cubic_term = 0.044715

N_Y, N_XL, N_XH, N_Z = 4, 2, 2, 32
TOK = 384
HALF = 192
HID = 256
ROWS = 12


def gelu_parts(value):
    square = value * value
    tangent = jnp.tanh(sqrt_two_pi * value * (1.0 + cubic_term * square))
    upper = 0.5 * (1.0 + tangent)
    gradient = upper + 0.5 * value * (1.0 - tangent * tangent) * sqrt_two_pi * (
        1.0 + 3.0 * cubic_term * square
    )
    return value * upper, gradient


def nn(a, b):
    return jnp.dot(a, b, preferred_element_type=F32)


def nt(a, b):
    return lax.dot_general(a, b, (((1,), (1,)), ((), ())), preferred_element_type=F32)


class Names:
    def __init__(self):
        self.of = {}

    def __call__(self, *name):
        return self.of.setdefault(name, len(self.of))


N_SEM = 96


def kernel(
    inputs, out_grad, w_in, w_out, in_keep, out_keep,
    o_in, o_out, o_x,
    acts, win, wout, win_l, wout_l, win_s, wout_s, kin, kout, acts_t, pre, ag,
    v_in, v_out, ya_in, yb_out, y1_in, y1_out, y3_in, y3_out, s_in, s_out, x_in, x_out,
    q_b, q_r, q_s, z_r, f_s, f_r,
    send_sem, recv_sem, local_sem, relay_sem,
):
    row, col = lax.axis_index("row"), lax.axis_index("col")
    y, xl = row // N_XL, row % N_XL
    xh, z, k = col // (2 * N_Z), (col // 2) % N_Z, col % 2
    x = 2 * xh + xl
    h = z % 2
    pair = z + 1 - 2 * h

    def dev(y=y, x=x, z=z, k=k):
        return (y * N_XL + x % 2, ((x // 2) * N_Z + z) * 2 + k)

    def up(d):
        return (y + d) % N_Y

    def xr(d):
        return (x + d) % 4

    def along_z(d):
        return dev(z=(z + d + N_Z) % N_Z)

    core = dev(k=1 - k)
    inner = dev(x=2 * xh + 1 - xl)
    ydev = {d: dev(y=up(d)) for d in (1, 2, 3)}
    xdev = {d: dev(x=xr(d)) for d in (1, 3)}
    near = {
        (e, f): dev(x=xr(e), z=pair if f else z) for f in (0, 1) for e in range(4) if e or f
    }

    def owner(j):
        return dev(
            y=2 * (1 - xh) + k,
            x=2 * (y // 2) + xl,
            z=8 * (j // 4) + 4 * h + 2 * (y % 2) + j % 4 // 2,
            k=j % 2,
        )

    barrier = pltpu.get_barrier_semaphore()
    partners = [core, *ydev.values(), *near.values(), along_z(2 * h - 1)]
    partners += [dev(y=2 * xh + i, x=2 * (1 - y // 2) + xl, k=y % 2) for i in (0, 1)]
    for device in partners:
        pl.semaphore_signal(barrier, inc=1, device_id=device, device_id_type=MESH)

    names = Names()
    sent = []

    def copy(src, dst, name, device):
        i = names(*name)
        return pltpu.make_async_remote_copy(
            src_ref=src, dst_ref=dst, send_sem=send_sem.at[i], recv_sem=recv_sem.at[i],
            device_id=device, device_id_type=MESH,
        )

    def send(src, dst, name, device):
        c = copy(src, dst, name, device)
        c.start()
        sent.append(c)

    def arrived(dst, name):
        copy(dst, dst, name, core).wait_recv()

    def tell(r):
        for d in (-(1, 1, 2, 4, 8)[r], (1, 1, 2, 4, 8)[r]):
            pl.semaphore_signal(
                relay_sem.at[r], inc=1, device_id=along_z(d), device_id_type=MESH
            )

    def heard(r):
        pl.semaphore_wait(relay_sem.at[r], 2)

    local = [
        pltpu.make_async_copy(src, dst, local_sem.at[i])
        for i, (src, dst) in enumerate(
            ((w_in, win_l), (w_out, wout_l), (in_keep, kin), (out_keep, kout))
        )
    ]
    for c in local:
        c.start()
    for c in local:
        c.wait()

    def pruned_in(j):
        at = pl.ds(pl.multiple_of(j * BLOCK, BLOCK), BLOCK)
        return (win_l[:, at].astype(F32) * kin[0, j].astype(F32)).astype(BF)

    def pruned_out(j):
        at = pl.ds(pl.multiple_of(j * BLOCK, BLOCK), BLOCK)
        return (wout_l[at, :].astype(F32) * kout[0, j].astype(F32)).astype(BF)

    for jj in range(2):
        part = pl.ds(BLOCK * jj, BLOCK)
        win_s[:, part] = pruned_in(2 * (1 - xl) + jj)
        wout_s[part, :] = pruned_out(2 * (1 - xl) + jj)
        win[0, 0:BLOCK, part] = pruned_in(2 * xl + jj)
        wout[0, part, 0:BLOCK] = pruned_out(2 * xl + jj)

    pl.semaphore_wait(barrier, len(partners))

    def runs(half):
        return pl.ds(4 * half, 4)

    mine, other = runs(xh), runs(1 - xh)

    def tokens(array, of_y, half):
        return array.at[of_y // 2, :, half, of_y % 2]

    lo, hi = pl.ds(0, BLOCK), pl.ds(BLOCK, BLOCK)

    def win_at(d, p):
        return win.at[d, pl.ds(BLOCK * p, BLOCK), :]

    def wout_at(d, p):
        return wout.at[d, :, pl.ds(BLOCK * p, BLOCK)]

    def own_tokens(array):
        return [
            pltpu.make_async_copy(
                tokens(array, y, half), acts.at[k, 0, runs(half), :, lo], local_sem.at[4 + half]
            )
            for half in (0, 1)
        ]

    def first_copies(array):
        along_y = [
            copy(
                tokens(array, up(d), xh), acts.at[k, 4 - d, mine, :, lo], ("ay", 4 - d), ydev[d]
            )
            for d in (1, 3, 2)
        ]
        along_x = [
            copy(tokens(array, y, xh), acts.at[k, 0, mine, :, hi], ("ax", 0, 4 - d), xdev[d])
            for d in (1, 3)
        ]
        return along_y + along_x

    send(win_s, win_at(0, 1), ("wx_in",), inner)
    send(wout_s, wout_at(0, 1), ("wx_out",), inner)

    for i, array in enumerate((inputs, out_grad)):

        @pl.when(k == i)
        def _():
            for c in first_copies(array) + own_tokens(array):
                c.start()

    sent += first_copies(inputs)

    def spread(p):
        for d in (1, 3):
            send(win_at(0, p), win_at(4 - d, p), ("wy_in", 4 - d, p), ydev[d])
            send(wout_at(0, p), wout_at(4 - d, p), ("wy_out", 4 - d, p), ydev[d])

    spread(0)
    tell(0)

    def pass_on(p):
        arrived(win_at(3, p), ("wy_in", 3, p))
        send(win_at(3, p), win_at(2, p), ("wf_in", p), ydev[1])
        arrived(wout_at(1, p), ("wy_out", 1, p))
        send(wout_at(1, p), wout_at(2, p), ("wf_out", p), ydev[3])

    def token_half(e):
        return runs(xr(e) // 2)

    def from_x(d, e):
        return acts.at[k, d, token_half(e), :, hi]

    def both_x(d):
        for e in (1, 3):
            arrived(from_x(d, e), ("ax", d, e))
        if d == 2:
            away = 1 + 2 * k
            half = runs(((x + 4 - away) % 4) // 2)
            send(
                acts.at[k, d, half, :, hi],
                acts.at[k, d, half, :, lo],
                ("af", d),
                dev(x=(x + away) % 4),
            )
        elif d:
            send(from_x(d, d), acts.at[k, d, token_half(d), :, lo], ("af", d), xdev[4 - d])

    def to_core(d):
        if d:
            arrived(acts.at[k, d, other, :, lo], ("af", d))
        send(acts.at[k, d], acts.at[k, d], ("ac", d), core)

    def flat(i, d):
        return acts[i, d].reshape(TOK, 2 * BLOCK)

    def products(d):
        for p in (0, 1):
            if d == 1:
                arrived(win_at(1, p), ("wy_in", 1, p))
            if d == 3:
                arrived(wout_at(3, p), ("wy_out", 3, p))
            if d == 2:
                arrived(win_at(2, p), ("wf_in", p))
                arrived(wout_at(2, p), ("wf_out", p))
        arrived(acts.at[1 - k, d], ("ac", d))
        a, b = nn(flat(0, d), win[d]), nt(flat(1, d), wout[d])
        if d == 0:
            pre[...], ag[...] = a, b
        else:
            pre[...] += a
            ag[...] += b

    for d in (3, 1, 2):
        here = acts.at[k, d, mine, :, lo]
        arrived(here, ("ay", d))
        for e in (1, 3):
            send(here, acts.at[k, d, mine, :, hi], ("ax", d, 4 - e), xdev[e])
        if d == 3:
            heard(0)
            tell(1)

    arrived(win_at(0, 1), ("wx_in",))
    arrived(wout_at(0, 1), ("wx_out",))
    spread(1)
    heard(1)
    tell(2)
    pass_on(0)
    for c in own_tokens(inputs):
        c.wait()
    both_x(0)
    to_core(0)
    both_x(3)
    heard(2)
    tell(3)
    both_x(1)
    pass_on(1)
    both_x(2)
    to_core(3)
    products(0)
    to_core(1)
    products(3)
    to_core(2)
    heard(3)
    tell(4)
    products(1)
    products(2)

    activated, gradient = gelu_parts(pre[...])
    pg = (ag[...] * gradient).astype(BF)
    act_t = activated.astype(BF).T

    def slices(s, i):
        of_y = s + 2 * i
        q = nt(pg, win[(of_y - y + N_Y) % N_Y]).astype(BF)
        q_b[s, 2 * (1 - i) + xl] = q[:, 0:BLOCK]
        q_b[s, 2 * (1 - i) + 1 - xl] = q[:, BLOCK:]

    for i in (0, 1):
        slices(1 - k, i)
        half = pl.ds(2 * (1 - i), 2)
        send(q_b.at[1 - k, half], q_r.at[half], ("q", i), core)
    for i in (0, 1):
        slices(k, i)

    def rows_of(f):
        return pl.ds(pl.multiple_of(HALF * ((h + f) % 2), HALF), HALF)

    for i in (0, 1):
        half = pl.ds(2 * (1 - i), 2)
        arrived(q_r.at[half], ("q", i))
        q_s[half] = (q_b[k, half].astype(F32) + q_r[half].astype(F32)).astype(BF)

    for e, f in ((2, 1), (1, 1), (3, 1), (2, 0), (1, 0), (3, 0), (0, 1)):
        send(
            q_s.at[xr(e), rows_of(f)], z_r.at[4 * f + (4 - e) % 4], ("z", (4 - e) % 4, f), near[e, f]
        )
    total = q_s[x, rows_of(0)].astype(F32)
    for e, f in ((1, 0), (3, 0), (0, 1), (1, 1), (3, 1), (2, 0), (2, 1)):
        arrived(z_r.at[4 * f + e], ("z", e, f))
        total += z_r[4 * f + e].astype(F32)

    f_s[...] = jnp.zeros_like(f_s)
    for j in range(16):
        f_s[j, 0:ROWS] = total[ROWS * j : ROWS * (j + 1)].astype(BF)
    heard(4)
    group = z // 2
    first = [names("f", g) for g in range(16)][0]
    for j in range(16):
        c = pltpu.make_async_remote_copy(
            src_ref=f_s.at[j], dst_ref=f_r.at[group], send_sem=send_sem.at[first + j],
            recv_sem=recv_sem.at[first + group], device_id=owner(j), device_id_type=MESH,
        )
        c.start()
        sent.append(c)

    def grads(d):
        acts_t[...] = flat(0, d).T
        v_in[d] = nn(acts_t[...], pg).astype(BF)
        v_out[d] = nn(act_t, flat(1, d)).astype(BF)

    grads(2)
    send(v_in.at[2], ya_in, ("ya",), ydev[1])
    send(v_out.at[2], yb_out, ("yb",), ydev[3])
    grads(1)
    send(v_out.at[1], y1_out, ("y1_out",), ydev[1])
    grads(3)
    send(v_in.at[3], y3_in, ("y3_in",), ydev[3])
    grads(0)

    arrived(ya_in, ("ya",))
    v_in[1] = (v_in[1].astype(F32) + ya_in[...].astype(F32)).astype(BF)
    send(v_in.at[1], y1_in, ("y1_in",), ydev[1])
    arrived(yb_out, ("yb",))
    v_out[3] = (v_out[3].astype(F32) + yb_out[...].astype(F32)).astype(BF)
    send(v_out.at[3], y3_out, ("y3_out",), ydev[3])

    arrived(y1_in, ("y1_in",))
    arrived(y3_in, ("y3_in",))
    s_in[...] = v_in[0].astype(F32) + y1_in[...].astype(F32) + y3_in[...].astype(F32)
    x_in[0] = s_in[BLOCK:].astype(BF)
    send(x_in.at[0], x_in.at[1], ("gx_in",), inner)
    arrived(y1_out, ("y1_out",))
    arrived(y3_out, ("y3_out",))
    s_out[...] = v_out[0].astype(F32) + y1_out[...].astype(F32) + y3_out[...].astype(F32)
    x_out[0] = s_out[:, BLOCK:].astype(BF)
    send(x_out.at[0], x_out.at[1], ("gx_out",), inner)

    def store_in(j, value):
        at = pl.ds(pl.multiple_of(j * BLOCK, BLOCK), BLOCK)
        o_in[:, at] = value * kin[0, j].astype(F32)

    def store_out(j, value):
        at = pl.ds(pl.multiple_of(j * BLOCK, BLOCK), BLOCK)
        o_out[at, :] = value * kout[0, j].astype(F32)

    cuts = [pl.ds(BLOCK * jj, BLOCK) for jj in (0, 1)]
    for jj, cut in enumerate(cuts):
        store_in(2 * xl + jj, s_in[0:BLOCK, cut])
        store_out(2 * xl + jj, s_out[cut, 0:BLOCK])
    arrived(x_in.at[1], ("gx_in",))
    for jj, cut in enumerate(cuts):
        store_in(2 * (1 - xl) + jj, x_in[1, :, cut].astype(F32))
    arrived(x_out.at[1], ("gx_out",))
    for jj, cut in enumerate(cuts):
        store_out(2 * (1 - xl) + jj, x_out[1, cut, :].astype(F32))

    for c in sent:
        c.wait_send()

    for g in range(16):
        arrived(f_r.at[g], ("f", g))
    last = f_r[0].astype(F32)
    for g in range(1, 16):
        last += f_r[g].astype(F32)
    o_x[...] = last[0:ROWS]


def write_out(a, b, c, a_out, b_out, c_out, sem):
    pairs = ((a, a_out), (b, b_out), (c, c_out))
    copies = [pltpu.make_async_copy(src, dst, sem.at[i]) for i, (src, dst) in enumerate(pairs)]
    for one in copies:
        one.start()
    for one in copies:
        one.wait()


def per_device(inputs, out_grad, w_in, w_out, in_keep, out_keep):
    arrays = [
        pltpu.with_memory_space_constraint(array, pltpu.HBM)
        for array in (
            inputs.reshape(2, 4, 2, 2, TOK // 8, BLOCK),
            out_grad.reshape(2, 4, 2, 2, TOK // 8, BLOCK),
            w_in,
            w_out,
            in_keep,
            out_keep.reshape(1, -1),
        )
    ]
    vmem = pl.BlockSpec(memory_space=pltpu.VMEM)
    hbm = pl.BlockSpec(memory_space=pltpu.HBM)
    B, H, V = BLOCK, HID, pltpu.VMEM
    results = pl.pallas_call(
        kernel,
        out_shape=(
            jax.ShapeDtypeStruct((B, 2 * H), F32),
            jax.ShapeDtypeStruct((2 * H, B), F32),
            jax.ShapeDtypeStruct((ROWS, B), F32),
        ),
        in_specs=[hbm] * 6,
        out_specs=[vmem, vmem, vmem],
        scratch_shapes=[
            V((2, 4, 8, TOK // 8, 2 * B), BF),
            V((4, 2 * B, H), BF),
            V((4, H, 2 * B), BF),
            V((B, 2 * H), BF),
            V((2 * H, B), BF),
            V((B, H), BF),
            V((H, B), BF),
            pltpu.SMEM((1, 4), jnp.int32),
            pltpu.SMEM((1, 4), jnp.int32),
            V((2 * B, TOK), BF),
            V((TOK, H), F32),
            V((TOK, H), F32),
            V((4, 2 * B, H), BF),
            V((4, H, 2 * B), BF),
            V((2 * B, H), BF),
            V((H, 2 * B), BF),
            V((2 * B, H), BF),
            V((H, 2 * B), BF),
            V((2 * B, H), BF),
            V((H, 2 * B), BF),
            V((2 * B, H), F32),
            V((H, 2 * B), F32),
            V((2, B, H), BF),
            V((2, H, B), BF),
            V((2, 4, TOK, B), BF),
            V((4, TOK, B), BF),
            V((4, TOK, B), BF),
            V((8, HALF, B), BF),
            V((16, 16, B), BF),
            V((16, 16, B), BF),
            pltpu.SemaphoreType.DMA((N_SEM,)),
            pltpu.SemaphoreType.DMA((N_SEM,)),
            pltpu.SemaphoreType.DMA((6,)),
            pltpu.SemaphoreType.REGULAR((5,)),
        ],
        compiler_params=pltpu.CompilerParams(
            collective_id=0, has_side_effects=True, vmem_limit_bytes=48 * 1024 * 1024
        ),
    )(*arrays)
    return pl.pallas_call(
        write_out,
        out_shape=tuple(jax.ShapeDtypeStruct(r.shape, r.dtype) for r in results),
        in_specs=[vmem] * 3,
        out_specs=[hbm] * 3,
        scratch_shapes=[pltpu.SemaphoreType.DMA((3,))],
        compiler_params=pltpu.CompilerParams(vmem_limit_bytes=4 * 1024 * 1024),
    )(*results)


def solution(mesh):
    return jax.shard_map(
        per_device,
        mesh=mesh,
        in_specs=(
            P(None, "row"),
            P(None, "row"),
            P("row", "col"),
            P("col", "row"),
            P("row", "col"),
            P("col", "row"),
        ),
        out_specs=(P("row", "col"), P("col", "row"), P("col", "row")),
        check_vma=False,
    )
```

```python
import functools

import jax
import jax.numpy as jnp
from jax import lax
from jax.experimental import pallas as pl
from jax.experimental.pallas import tpu as pltpu
from jax.sharding import PartitionSpec as P

MESH = pl.DeviceIdType.MESH
BLOCK = 128
BF = jnp.bfloat16
F32 = jnp.float32

sqrt_two_pi = 0.7978845608028654
cubic_term = 0.044715

N_Y, N_XL, N_XH, N_Z = 4, 2, 2, 32
TOK = 384
HALF = 192
HID = 256
ROWS = 12


def tangent_of(value):
    return jnp.tanh(sqrt_two_pi * value * (1.0 + cubic_term * value * value))


def gelu(value):
    return 0.5 * value * (1.0 + tangent_of(value))


def gelu_slope(value):
    t = tangent_of(value)
    return 0.5 * (1.0 + t) + 0.5 * value * (1.0 - t * t) * sqrt_two_pi * (
        1.0 + 3.0 * cubic_term * value * value
    )


def nn(a, b):
    return jnp.dot(a, b, preferred_element_type=F32)


def nt(a, b):
    return lax.dot_general(a, b, (((1,), (1,)), ((), ())), preferred_element_type=F32)


class Names:
    def __init__(self):
        self.of = {}

    def __call__(self, *name):
        return self.of.setdefault(name, len(self.of))


N_SEM = 96


def kernel(
    inputs, out_grad, w_in, w_out, in_keep, out_keep,
    o_in, o_out, o_x,
    acts, win, wout, win_l, wout_l, win_s, wout_s, kin, kout, acts_t, pre, ag,
    v_in, v_out, ya_in, yb_out, y1_in, y1_out, y3_in, y3_out, s_in, s_out, x_in, x_out,
    q_o, q_m, q_r, q_s, z_r, f_s, f_r,
    send_sem, recv_sem, local_sem, relay_sem,
):
    row, col = lax.axis_index("row"), lax.axis_index("col")
    y, xl = row // N_XL, row % N_XL
    xh, z, k = col // (2 * N_Z), (col // 2) % N_Z, col % 2
    x = 2 * xh + xl
    h = z % 2
    pair = z + 1 - 2 * h

    def dev(y=y, x=x, z=z, k=k):
        return (y * N_XL + x % 2, ((x // 2) * N_Z + z) * 2 + k)

    def up(d):
        return (y + d) % N_Y

    def xr(d):
        return (x + d) % 4

    def along_z(d):
        return dev(z=(z + d + N_Z) % N_Z)

    core = dev(k=1 - k)
    inner = dev(x=2 * xh + 1 - xl)
    ydev = {d: dev(y=up(d)) for d in (1, 2, 3)}
    xdev = {d: dev(x=xr(d)) for d in (1, 3)}
    near = {
        (e, f): dev(x=xr(e), z=pair if f else z) for f in (0, 1) for e in range(4) if e or f
    }

    def owner(j):
        return dev(y=up(2 * h + k), z=8 * (j // 4) + 2 * y + j % 4 // 2, k=j % 2)

    barrier = pltpu.get_barrier_semaphore()
    partners = [core, *ydev.values(), *near.values(), along_z(2 * h - 1)]
    partners += [dev(y=up(d), k=1 - k) for d in (1, 2, 3)]
    for device in partners:
        pl.semaphore_signal(barrier, inc=1, device_id=device, device_id_type=MESH)

    names = Names()
    sent = []

    def copy(src, dst, name, device):
        i = names(*name)
        return pltpu.make_async_remote_copy(
            src_ref=src, dst_ref=dst, send_sem=send_sem.at[i], recv_sem=recv_sem.at[i],
            device_id=device, device_id_type=MESH,
        )

    def send(src, dst, name, device):
        c = copy(src, dst, name, device)
        c.start()
        sent.append(c)

    def arrived(dst, name):
        copy(dst, dst, name, core).wait_recv()

    def tell(r):
        for d in (-(1, 1, 2, 4, 8)[r], (1, 1, 2, 4, 8)[r]):
            pl.semaphore_signal(
                relay_sem.at[r], inc=1, device_id=along_z(d), device_id_type=MESH
            )

    def heard(r):
        pl.semaphore_wait(relay_sem.at[r], 2)

    local = [
        pltpu.make_async_copy(src, dst, local_sem.at[i])
        for i, (src, dst) in enumerate(
            ((w_in, win_l), (w_out, wout_l), (in_keep, kin), (out_keep, kout))
        )
    ]
    for c in local:
        c.start()
    for c in local:
        c.wait()

    def pruned_in(j):
        at = pl.ds(pl.multiple_of(j * BLOCK, BLOCK), BLOCK)
        return (win_l[:, at].astype(F32) * kin[0, j].astype(F32)).astype(BF)

    def pruned_out(j):
        at = pl.ds(pl.multiple_of(j * BLOCK, BLOCK), BLOCK)
        return (wout_l[at, :].astype(F32) * kout[0, j].astype(F32)).astype(BF)

    for jj in range(2):
        part = pl.ds(BLOCK * jj, BLOCK)
        win_s[:, part] = pruned_in(2 * (1 - xl) + jj)
        wout_s[part, :] = pruned_out(2 * (1 - xl) + jj)
        win[0, 0:BLOCK, part] = pruned_in(2 * xl + jj)
        wout[0, part, 0:BLOCK] = pruned_out(2 * xl + jj)

    pl.semaphore_wait(barrier, len(partners))

    def runs(half):
        return pl.ds(4 * half, 4)

    mine, other = runs(xh), runs(1 - xh)

    def tokens(array, of_y, half):
        return array.at[half, :, of_y]

    lo, hi = pl.ds(0, BLOCK), pl.ds(BLOCK, BLOCK)

    def win_at(d, p):
        return win.at[d, pl.ds(BLOCK * p, BLOCK), :]

    def wout_at(d, p):
        return wout.at[d, :, pl.ds(BLOCK * p, BLOCK)]

    def own_tokens(array):
        return [
            pltpu.make_async_copy(
                tokens(array, y, half), acts.at[k, 0, runs(half), :, lo], local_sem.at[4 + half]
            )
            for half in (0, 1)
        ]

    def first_copies(array):
        along_y = [
            copy(
                tokens(array, up(d), xh), acts.at[k, 4 - d, mine, :, lo], ("ay", 4 - d), ydev[d]
            )
            for d in (2, 1, 3)
        ]
        along_x = [
            copy(tokens(array, y, xh), acts.at[k, 0, mine, :, hi], ("ax", 0, 4 - d), xdev[d])
            for d in (1, 3)
        ]
        return along_y + along_x

    send(win_s, win_at(0, 1), ("wx_in",), inner)
    send(wout_s, wout_at(0, 1), ("wx_out",), inner)

    for i, array in enumerate((inputs, out_grad)):

        @pl.when(k == i)
        def _():
            for c in first_copies(array) + own_tokens(array):
                c.start()

    sent += first_copies(inputs)

    def spread(p):
        for d in (1, 3):
            send(win_at(0, p), win_at(4 - d, p), ("wy_in", 4 - d, p), ydev[d])
            send(wout_at(0, p), wout_at(4 - d, p), ("wy_out", 4 - d, p), ydev[d])

    spread(0)
    tell(0)

    def pass_on(p):
        arrived(win_at(3, p), ("wy_in", 3, p))
        send(win_at(3, p), win_at(2, p), ("wf_in", p), ydev[1])
        arrived(wout_at(1, p), ("wy_out", 1, p))
        send(wout_at(1, p), wout_at(2, p), ("wf_out", p), ydev[3])

    def token_half(e):
        return runs(xr(e) // 2)

    def from_x(d, e):
        return acts.at[k, d, token_half(e), :, hi]

    def both_x(d):
        for e in (1, 3):
            arrived(from_x(d, e), ("ax", d, e))
        if d == 2:
            away = 1 + 2 * k
            half = runs(((x + 4 - away) % 4) // 2)
            send(
                acts.at[k, d, half, :, hi],
                acts.at[k, d, half, :, lo],
                ("af", d),
                dev(x=(x + away) % 4),
            )
        elif d:
            send(from_x(d, d), acts.at[k, d, token_half(d), :, lo], ("af", d), xdev[4 - d])

    def to_core(d):
        if d:
            arrived(acts.at[k, d, other, :, lo], ("af", d))
        send(acts.at[k, d], acts.at[k, d], ("ac", d), core)

    def flat(i, d):
        return acts[i, d].reshape(TOK, 2 * BLOCK)

    def products(d):
        for p in (0, 1):
            if d == 1:
                arrived(win_at(1, p), ("wy_in", 1, p))
            if d == 3:
                arrived(wout_at(3, p), ("wy_out", 3, p))
            if d == 2:
                arrived(win_at(2, p), ("wf_in", p))
                arrived(wout_at(2, p), ("wf_out", p))
        arrived(acts.at[1 - k, d], ("ac", d))
        a, b = nn(flat(0, d), win[d]), nt(flat(1, d), wout[d])
        if d == 0:
            pre[...], ag[...] = a, b
        else:
            pre[...] += a
            ag[...] += b

    for d in (3, 1, 2):
        here = acts.at[k, d, mine, :, lo]
        arrived(here, ("ay", d))
        for e in (1, 3):
            send(here, acts.at[k, d, mine, :, hi], ("ax", d, 4 - e), xdev[e])
        if d == 3:
            heard(0)
            tell(1)

    arrived(win_at(0, 1), ("wx_in",))
    arrived(wout_at(0, 1), ("wx_out",))
    spread(1)
    heard(1)
    tell(2)
    pass_on(0)
    for c in own_tokens(inputs):
        c.wait()
    both_x(0)
    to_core(0)
    both_x(3)
    heard(2)
    tell(3)
    both_x(1)
    pass_on(1)
    both_x(2)
    to_core(3)
    products(0)
    to_core(1)
    products(3)
    to_core(2)
    heard(3)
    tell(4)
    products(1)
    products(2)

    pg = (ag[...] * gelu_slope(pre[...])).astype(BF)

    def slices(buffer, to_h, d):
        q = nt(pg, win[d]).astype(BF)
        buffer[to_h, 0] = q[:, 0:BLOCK]
        buffer[to_h, 1] = q[:, BLOCK:]

    def parity(f):
        return (h + f) % 2

    for f in (1, 0):
        slices(q_o, parity(f), 2 * parity(f) + 1 - k)
        send(q_o.at[parity(f)], q_r.at[parity(f)], ("q", f), core)
    for f in (1, 0):
        slices(q_m, parity(f), 2 * parity(f) + k)

    def rows_of(e):
        return pl.ds(pl.multiple_of(HALF * (xr(e) // 2), HALF), HALF)

    for f in (1, 0):
        to_h = parity(f)
        arrived(q_r.at[to_h], ("q", f))
        q_s[to_h] = (q_m[to_h].astype(F32) + q_r[to_h].astype(F32)).astype(BF)
        for e in (2, 1, 3, 0):
            if e or f:
                send(
                    q_s.at[to_h, e % 2, rows_of(e)],
                    z_r.at[4 * f + (4 - e) % 4],
                    ("z", (4 - e) % 4, f),
                    near[e, f],
                )
    total = q_s[h, 0, rows_of(0)].astype(F32)
    for e, f in ((0, 1), (1, 1), (3, 1), (1, 0), (3, 0), (2, 1), (2, 0)):
        arrived(z_r.at[4 * f + e], ("z", e, f))
        total += z_r[4 * f + e].astype(F32)

    f_s[...] = jnp.zeros_like(f_s)
    for j in range(16):
        f_s[j, 0:ROWS] = total[ROWS * j : ROWS * (j + 1)].astype(BF)
    heard(4)
    group = z // 2
    first = [names("f", g) for g in range(16)][0]
    own_owner = (h == 0) & (k == 0) & (z % 8 == 2 * y)

    def unless(own, act):
        if own is None:
            act()
        else:
            pl.when(jnp.logical_not(own))(act)

    far = []
    for j in range(16):
        own = own_owner & (z // 8 == j // 4) if j % 4 == 0 else None
        c = pltpu.make_async_remote_copy(
            src_ref=f_s.at[j], dst_ref=f_r.at[group], send_sem=send_sem.at[first + j],
            recv_sem=recv_sem.at[first + group], device_id=owner(j), device_id_type=MESH,
        )
        unless(own, c.start)
        far.append((own, c.wait_send))
        if own is not None:

            @pl.when(own)
            def _():
                f_r[group] = f_s[j]

    act_t = gelu(pre[...]).astype(BF).T

    def grads(d):
        acts_t[...] = flat(0, d).T
        v_in[d] = nn(acts_t[...], pg).astype(BF)
        v_out[d] = nn(act_t, flat(1, d)).astype(BF)

    grads(2)
    send(v_in.at[2], ya_in, ("ya",), ydev[1])
    send(v_out.at[2], yb_out, ("yb",), ydev[3])
    grads(1)
    send(v_out.at[1], y1_out, ("y1_out",), ydev[1])
    grads(3)
    send(v_in.at[3], y3_in, ("y3_in",), ydev[3])
    grads(0)

    arrived(ya_in, ("ya",))
    v_in[1] = (v_in[1].astype(F32) + ya_in[...].astype(F32)).astype(BF)
    send(v_in.at[1], y1_in, ("y1_in",), ydev[1])
    arrived(yb_out, ("yb",))
    v_out[3] = (v_out[3].astype(F32) + yb_out[...].astype(F32)).astype(BF)
    send(v_out.at[3], y3_out, ("y3_out",), ydev[3])

    arrived(y1_in, ("y1_in",))
    arrived(y3_in, ("y3_in",))
    s_in[...] = v_in[0].astype(F32) + y1_in[...].astype(F32) + y3_in[...].astype(F32)
    x_in[0] = s_in[BLOCK:].astype(BF)
    send(x_in.at[0], x_in.at[1], ("gx_in",), inner)
    arrived(y1_out, ("y1_out",))
    arrived(y3_out, ("y3_out",))
    s_out[...] = v_out[0].astype(F32) + y1_out[...].astype(F32) + y3_out[...].astype(F32)
    x_out[0] = s_out[:, BLOCK:].astype(BF)
    send(x_out.at[0], x_out.at[1], ("gx_out",), inner)

    def store_in(j, value):
        at = pl.ds(pl.multiple_of(j * BLOCK, BLOCK), BLOCK)
        o_in[:, at] = value * kin[0, j].astype(F32)

    def store_out(j, value):
        at = pl.ds(pl.multiple_of(j * BLOCK, BLOCK), BLOCK)
        o_out[at, :] = value * kout[0, j].astype(F32)

    cuts = [pl.ds(BLOCK * jj, BLOCK) for jj in (0, 1)]
    for jj, cut in enumerate(cuts):
        store_in(2 * xl + jj, s_in[0:BLOCK, cut])
        store_out(2 * xl + jj, s_out[cut, 0:BLOCK])
    arrived(x_in.at[1], ("gx_in",))
    for jj, cut in enumerate(cuts):
        store_in(2 * (1 - xl) + jj, x_in[1, :, cut].astype(F32))
    arrived(x_out.at[1], ("gx_out",))
    for jj, cut in enumerate(cuts):
        store_out(2 * (1 - xl) + jj, x_out[1, cut, :].astype(F32))

    for c in sent:
        c.wait_send()
    for own, wait in far:
        unless(own, wait)

    for g in range(16):
        unless(own_owner & (group == g), functools.partial(arrived, f_r.at[g], ("f", g)))
    last = f_r[0].astype(F32)
    for g in range(1, 16):
        last += f_r[g].astype(F32)
    o_x[...] = last[0:ROWS]


def write_out(a, b, c, a_out, b_out, c_out, sem):
    pairs = ((a, a_out), (b, b_out), (c, c_out))
    copies = [pltpu.make_async_copy(src, dst, sem.at[i]) for i, (src, dst) in enumerate(pairs)]
    for one in copies:
        one.start()
    for one in copies:
        one.wait()


def per_device(inputs, out_grad, w_in, w_out, in_keep, out_keep):
    arrays = [
        pltpu.with_memory_space_constraint(array, pltpu.HBM)
        for array in (
            inputs.reshape(2, 4, 4, TOK // 8, BLOCK),
            out_grad.reshape(2, 4, 4, TOK // 8, BLOCK),
            w_in,
            w_out,
            in_keep,
            out_keep.reshape(1, -1),
        )
    ]
    vmem = pl.BlockSpec(memory_space=pltpu.VMEM)
    hbm = pl.BlockSpec(memory_space=pltpu.HBM)
    B, H, V = BLOCK, HID, pltpu.VMEM
    results = pl.pallas_call(
        kernel,
        out_shape=(
            jax.ShapeDtypeStruct((B, 2 * H), F32),
            jax.ShapeDtypeStruct((2 * H, B), F32),
            jax.ShapeDtypeStruct((ROWS, B), F32),
        ),
        in_specs=[hbm] * 6,
        out_specs=[vmem, vmem, vmem],
        scratch_shapes=[
            V((2, 4, 8, TOK // 8, 2 * B), BF),
            V((4, 2 * B, H), BF),
            V((4, H, 2 * B), BF),
            V((B, 2 * H), BF),
            V((2 * H, B), BF),
            V((B, H), BF),
            V((H, B), BF),
            pltpu.SMEM((1, 4), jnp.int32),
            pltpu.SMEM((1, 4), jnp.int32),
            V((2 * B, TOK), BF),
            V((TOK, H), F32),
            V((TOK, H), F32),
            V((4, 2 * B, H), BF),
            V((4, H, 2 * B), BF),
            V((2 * B, H), BF),
            V((H, 2 * B), BF),
            V((2 * B, H), BF),
            V((H, 2 * B), BF),
            V((2 * B, H), BF),
            V((H, 2 * B), BF),
            V((2 * B, H), F32),
            V((H, 2 * B), F32),
            V((2, B, H), BF),
            V((2, H, B), BF),
            V((2, 2, TOK, B), BF),
            V((2, 2, TOK, B), BF),
            V((2, 2, TOK, B), BF),
            V((2, 2, TOK, B), BF),
            V((8, HALF, B), BF),
            V((16, 16, B), BF),
            V((16, 16, B), BF),
            pltpu.SemaphoreType.DMA((N_SEM,)),
            pltpu.SemaphoreType.DMA((N_SEM,)),
            pltpu.SemaphoreType.DMA((6,)),
            pltpu.SemaphoreType.REGULAR((5,)),
        ],
        compiler_params=pltpu.CompilerParams(
            collective_id=0, has_side_effects=True, vmem_limit_bytes=48 * 1024 * 1024
        ),
    )(*arrays)
    return pl.pallas_call(
        write_out,
        out_shape=tuple(jax.ShapeDtypeStruct(r.shape, r.dtype) for r in results),
        in_specs=[vmem] * 3,
        out_specs=[hbm] * 3,
        scratch_shapes=[pltpu.SemaphoreType.DMA((3,))],
        compiler_params=pltpu.CompilerParams(vmem_limit_bytes=4 * 1024 * 1024),
    )(*results)


def solution(mesh):
    return jax.shard_map(
        per_device,
        mesh=mesh,
        in_specs=(
            P(None, "row"),
            P(None, "row"),
            P("row", "col"),
            P("col", "row"),
            P("row", "col"),
            P("col", "row"),
        ),
        out_specs=(P("row", "col"), P("col", "row"), P("col", "row")),
        check_vma=False,
    )
```

```python
import functools

import jax
import jax.numpy as jnp
from jax import lax
from jax.experimental import pallas as pl
from jax.experimental.pallas import tpu as pltpu
from jax.sharding import PartitionSpec as P

MESH = pl.DeviceIdType.MESH
BLOCK = 128
BF = jnp.bfloat16
F32 = jnp.float32

sqrt_two_pi = 0.7978845608028654
cubic_term = 0.044715

N_Y, N_XL, N_XH, N_Z = 4, 2, 2, 32
TOK = 384
HALF = 192
HID = 256
ROWS = 12


def tangent_of(value):
    return jnp.tanh(sqrt_two_pi * value * (1.0 + cubic_term * value * value))


def gelu(value):
    return 0.5 * value * (1.0 + tangent_of(value))


def gelu_slope(value):
    t = tangent_of(value)
    return 0.5 * (1.0 + t) + 0.5 * value * (1.0 - t * t) * sqrt_two_pi * (
        1.0 + 3.0 * cubic_term * value * value
    )


def nn(a, b):
    return jnp.dot(a, b, preferred_element_type=F32)


def nt(a, b):
    return lax.dot_general(a, b, (((1,), (1,)), ((), ())), preferred_element_type=F32)


class Names:
    def __init__(self):
        self.of = {}

    def __call__(self, *name):
        return self.of.setdefault(name, len(self.of))


N_SEM = 96


def kernel(
    inputs, out_grad, w_in, w_out, in_keep, out_keep,
    o_in, o_out, o_x,
    acts, win, wout, win_l, wout_l, win_s, wout_s, kin, kout, acts_t, pre, ag,
    v_in, v_out, ya_in, yb_out, y1_in, y1_out, y3_in, y3_out, s_in, s_out, x_in, x_out,
    q_o, q_m, q_r, q_s, z_r, f_s, f_r,
    send_sem, recv_sem, local_sem, relay_sem,
):
    row, col = lax.axis_index("row"), lax.axis_index("col")
    y, xl = row // N_XL, row % N_XL
    xh, z, k = col // (2 * N_Z), (col // 2) % N_Z, col % 2
    x = 2 * xh + xl
    h = z % 2
    pair = z + 1 - 2 * h

    def dev(y=y, x=x, z=z, k=k):
        return (y * N_XL + x % 2, ((x // 2) * N_Z + z) * 2 + k)

    def up(d):
        return (y + d) % N_Y

    def xr(d):
        return (x + d) % 4

    def along_z(d):
        return dev(z=(z + d + N_Z) % N_Z)

    core = dev(k=1 - k)
    inner = dev(x=2 * xh + 1 - xl)
    ydev = {d: dev(y=up(d)) for d in (1, 2, 3)}
    xdev = {d: dev(x=xr(d)) for d in (1, 3)}
    near = {
        (e, f): dev(x=xr(e), z=pair if f else z) for f in (0, 1) for e in range(4) if e or f
    }

    def owner(j):
        return dev(y=up(2 * h + k), z=8 * (j // 4) + 2 * y + j % 4 // 2, k=j % 2)

    barrier = pltpu.get_barrier_semaphore()
    partners = [core, *ydev.values(), *near.values(), along_z(2 * h - 1)]
    partners += [dev(y=up(d), k=1 - k) for d in (1, 2, 3)]
    for device in partners:
        pl.semaphore_signal(barrier, inc=1, device_id=device, device_id_type=MESH)

    names = Names()
    sent = []

    def copy(src, dst, name, device):
        i = names(*name)
        return pltpu.make_async_remote_copy(
            src_ref=src, dst_ref=dst, send_sem=send_sem.at[i], recv_sem=recv_sem.at[i],
            device_id=device, device_id_type=MESH,
        )

    def send(src, dst, name, device):
        c = copy(src, dst, name, device)
        c.start()
        sent.append(c)

    def arrived(dst, name):
        copy(dst, dst, name, core).wait_recv()

    def tell(r):
        for d in (-(1, 1, 2, 4, 8)[r], (1, 1, 2, 4, 8)[r]):
            pl.semaphore_signal(
                relay_sem.at[r], inc=1, device_id=along_z(d), device_id_type=MESH
            )

    def heard(r):
        pl.semaphore_wait(relay_sem.at[r], 2)

    local = [
        pltpu.make_async_copy(src, dst, local_sem.at[i])
        for i, (src, dst) in enumerate(
            ((w_in, win_l), (w_out, wout_l), (in_keep, kin), (out_keep, kout))
        )
    ]
    for c in local:
        c.start()
    pl.semaphore_wait(barrier, len(partners))

    def runs(half):
        return pl.ds(4 * half, 4)

    mine, other = runs(xh), runs(1 - xh)

    def tokens(array, of_y, half):
        return array.at[half, :, of_y]

    lo, hi = pl.ds(0, BLOCK), pl.ds(BLOCK, BLOCK)

    def win_at(d, p):
        return win.at[d, pl.ds(BLOCK * p, BLOCK), :]

    def wout_at(d, p):
        return wout.at[d, :, pl.ds(BLOCK * p, BLOCK)]

    def own_tokens(array):
        return [
            pltpu.make_async_copy(
                tokens(array, y, half), acts.at[k, 0, runs(half), :, lo], local_sem.at[4 + half]
            )
            for half in (0, 1)
        ]

    def first_copies(array):
        along_y = [
            copy(
                tokens(array, up(d), xh), acts.at[k, 4 - d, mine, :, lo], ("ay", 4 - d), ydev[d]
            )
            for d in (2, 1, 3)
        ]
        along_x = [
            copy(tokens(array, y, xh), acts.at[k, 0, mine, :, hi], ("ax", 0, 4 - d), xdev[d])
            for d in (1, 3)
        ]
        return along_y, along_x

    for i, array in enumerate((inputs, out_grad)):

        @pl.when(k == i)
        def _():
            for c in first_copies(array)[0] + own_tokens(array):
                c.start()

    for c in local:
        c.wait()

    def pruned_in(j):
        at = pl.ds(pl.multiple_of(j * BLOCK, BLOCK), BLOCK)
        return (win_l[:, at].astype(F32) * kin[0, j].astype(F32)).astype(BF)

    def pruned_out(j):
        at = pl.ds(pl.multiple_of(j * BLOCK, BLOCK), BLOCK)
        return (wout_l[at, :].astype(F32) * kout[0, j].astype(F32)).astype(BF)

    for jj in range(2):
        part = pl.ds(BLOCK * jj, BLOCK)
        win_s[:, part] = pruned_in(2 * (1 - xl) + jj)
        wout_s[part, :] = pruned_out(2 * (1 - xl) + jj)
        win[0, 0:BLOCK, part] = pruned_in(2 * xl + jj)
        wout[0, part, 0:BLOCK] = pruned_out(2 * xl + jj)

    send(win_s, win_at(0, 1), ("wx_in",), inner)
    send(wout_s, wout_at(0, 1), ("wx_out",), inner)

    for i, array in enumerate((inputs, out_grad)):

        @pl.when(k == i)
        def _():
            for c in first_copies(array)[1]:
                c.start()

    for copies in first_copies(inputs):
        sent += copies

    def spread(p):
        for d in (1, 3):
            send(win_at(0, p), win_at(4 - d, p), ("wy_in", 4 - d, p), ydev[d])
            send(wout_at(0, p), wout_at(4 - d, p), ("wy_out", 4 - d, p), ydev[d])

    spread(0)
    tell(0)

    def pass_on(p):
        arrived(win_at(3, p), ("wy_in", 3, p))
        send(win_at(3, p), win_at(2, p), ("wf_in", p), ydev[1])
        arrived(wout_at(1, p), ("wy_out", 1, p))
        send(wout_at(1, p), wout_at(2, p), ("wf_out", p), ydev[3])

    def token_half(e):
        return runs(xr(e) // 2)

    def from_x(d, e):
        return acts.at[k, d, token_half(e), :, hi]

    def both_x(d):
        for e in (1, 3):
            arrived(from_x(d, e), ("ax", d, e))
        if d == 2:
            away = 1 + 2 * k
            half = runs(((x + 4 - away) % 4) // 2)
            send(
                acts.at[k, d, half, :, hi],
                acts.at[k, d, half, :, lo],
                ("af", d),
                dev(x=(x + away) % 4),
            )
        elif d:
            send(from_x(d, d), acts.at[k, d, token_half(d), :, lo], ("af", d), xdev[4 - d])

    def to_core(d):
        if d:
            arrived(acts.at[k, d, other, :, lo], ("af", d))
        send(acts.at[k, d], acts.at[k, d], ("ac", d), core)

    def flat(i, d):
        return acts[i, d].reshape(TOK, 2 * BLOCK)

    def products(d):
        for p in (0, 1):
            if d == 1:
                arrived(win_at(1, p), ("wy_in", 1, p))
            if d == 3:
                arrived(wout_at(3, p), ("wy_out", 3, p))
            if d == 2:
                arrived(win_at(2, p), ("wf_in", p))
                arrived(wout_at(2, p), ("wf_out", p))
        arrived(acts.at[1 - k, d], ("ac", d))
        a, b = nn(flat(0, d), win[d]), nt(flat(1, d), wout[d])
        if d == 0:
            pre[...], ag[...] = a, b
        else:
            pre[...] += a
            ag[...] += b

    for d in (3, 1, 2):
        here = acts.at[k, d, mine, :, lo]
        arrived(here, ("ay", d))
        for e in (1, 3):
            send(here, acts.at[k, d, mine, :, hi], ("ax", d, 4 - e), xdev[e])
        if d == 3:
            heard(0)
            tell(1)

    arrived(win_at(0, 1), ("wx_in",))
    arrived(wout_at(0, 1), ("wx_out",))
    spread(1)
    heard(1)
    tell(2)
    pass_on(0)
    for c in own_tokens(inputs):
        c.wait()
    both_x(0)
    to_core(0)
    both_x(3)
    heard(2)
    tell(3)
    both_x(1)
    pass_on(1)
    both_x(2)
    to_core(3)
    products(0)
    to_core(1)
    products(3)
    to_core(2)
    heard(3)
    tell(4)
    products(1)
    products(2)

    pg = (ag[...] * gelu_slope(pre[...])).astype(BF)

    def slices(buffer, to_h, d):
        q = nt(pg, win[d]).astype(BF)
        buffer[to_h, 0] = q[:, 0:BLOCK]
        buffer[to_h, 1] = q[:, BLOCK:]

    def parity(f):
        return (h + f) % 2

    for f in (1, 0):
        slices(q_o, parity(f), 2 * parity(f) + 1 - k)
        send(q_o.at[parity(f)], q_r.at[parity(f)], ("q", f), core)
    for f in (1, 0):
        slices(q_m, parity(f), 2 * parity(f) + k)

    def rows_of(e):
        return pl.ds(pl.multiple_of(HALF * (xr(e) // 2), HALF), HALF)

    for f in (1, 0):
        to_h = parity(f)
        arrived(q_r.at[to_h], ("q", f))
        q_s[to_h] = (q_m[to_h].astype(F32) + q_r[to_h].astype(F32)).astype(BF)
        for e in (2, 1, 3, 0):
            if e or f:
                send(
                    q_s.at[to_h, e % 2, rows_of(e)],
                    z_r.at[4 * f + (4 - e) % 4],
                    ("z", (4 - e) % 4, f),
                    near[e, f],
                )
    total = q_s[h, 0, rows_of(0)].astype(F32)
    for e, f in ((0, 1), (1, 1), (3, 1), (1, 0), (3, 0), (2, 1), (2, 0)):
        arrived(z_r.at[4 * f + e], ("z", e, f))
        total += z_r[4 * f + e].astype(F32)

    f_s[...] = jnp.zeros_like(f_s)
    for j in range(16):
        f_s[j, 0:ROWS] = total[ROWS * j : ROWS * (j + 1)].astype(BF)
    heard(4)
    group = z // 2
    first = [names("f", g) for g in range(16)][0]
    own_owner = (h == 0) & (k == 0) & (z % 8 == 2 * y)

    def unless(own, act):
        if own is None:
            act()
        else:
            pl.when(jnp.logical_not(own))(act)

    far = []
    for j in range(16):
        own = own_owner & (z // 8 == j // 4) if j % 4 == 0 else None
        c = pltpu.make_async_remote_copy(
            src_ref=f_s.at[j], dst_ref=f_r.at[group], send_sem=send_sem.at[first + j],
            recv_sem=recv_sem.at[first + group], device_id=owner(j), device_id_type=MESH,
        )
        unless(own, c.start)
        far.append((own, c.wait_send))
        if own is not None:

            @pl.when(own)
            def _():
                f_r[group] = f_s[j]

    act_t = gelu(pre[...]).astype(BF).T

    def grads(d):
        acts_t[...] = flat(0, d).T
        v_in[d] = nn(acts_t[...], pg).astype(BF)
        v_out[d] = nn(act_t, flat(1, d)).astype(BF)

    grads(2)
    send(v_in.at[2], ya_in, ("ya",), ydev[1])
    send(v_out.at[2], yb_out, ("yb",), ydev[3])
    grads(1)
    send(v_out.at[1], y1_out, ("y1_out",), ydev[1])
    grads(3)
    send(v_in.at[3], y3_in, ("y3_in",), ydev[3])
    grads(0)

    arrived(ya_in, ("ya",))
    v_in[1] = (v_in[1].astype(F32) + ya_in[...].astype(F32)).astype(BF)
    send(v_in.at[1], y1_in, ("y1_in",), ydev[1])
    arrived(yb_out, ("yb",))
    v_out[3] = (v_out[3].astype(F32) + yb_out[...].astype(F32)).astype(BF)
    send(v_out.at[3], y3_out, ("y3_out",), ydev[3])

    arrived(y1_in, ("y1_in",))
    arrived(y3_in, ("y3_in",))
    s_in[...] = v_in[0].astype(F32) + y1_in[...].astype(F32) + y3_in[...].astype(F32)
    x_in[0] = s_in[BLOCK:].astype(BF)
    send(x_in.at[0], x_in.at[1], ("gx_in",), inner)
    arrived(y1_out, ("y1_out",))
    arrived(y3_out, ("y3_out",))
    s_out[...] = v_out[0].astype(F32) + y1_out[...].astype(F32) + y3_out[...].astype(F32)
    x_out[0] = s_out[:, BLOCK:].astype(BF)
    send(x_out.at[0], x_out.at[1], ("gx_out",), inner)

    def store_in(j, value):
        at = pl.ds(pl.multiple_of(j * BLOCK, BLOCK), BLOCK)
        o_in[:, at] = value * kin[0, j].astype(F32)

    def store_out(j, value):
        at = pl.ds(pl.multiple_of(j * BLOCK, BLOCK), BLOCK)
        o_out[at, :] = value * kout[0, j].astype(F32)

    cuts = [pl.ds(BLOCK * jj, BLOCK) for jj in (0, 1)]
    for jj, cut in enumerate(cuts):
        store_in(2 * xl + jj, s_in[0:BLOCK, cut])
        store_out(2 * xl + jj, s_out[cut, 0:BLOCK])
    arrived(x_in.at[1], ("gx_in",))
    for jj, cut in enumerate(cuts):
        store_in(2 * (1 - xl) + jj, x_in[1, :, cut].astype(F32))
    arrived(x_out.at[1], ("gx_out",))
    for jj, cut in enumerate(cuts):
        store_out(2 * (1 - xl) + jj, x_out[1, cut, :].astype(F32))

    for c in sent:
        c.wait_send()
    for own, wait in far:
        unless(own, wait)

    for g in range(16):
        unless(own_owner & (group == g), functools.partial(arrived, f_r.at[g], ("f", g)))
    last = f_r[0].astype(F32)
    for g in range(1, 16):
        last += f_r[g].astype(F32)
    o_x[...] = last[0:ROWS]


def write_out(a, b, c, a_out, b_out, c_out, sem):
    pairs = ((a, a_out), (b, b_out), (c, c_out))
    copies = [pltpu.make_async_copy(src, dst, sem.at[i]) for i, (src, dst) in enumerate(pairs)]
    for one in copies:
        one.start()
    for one in copies:
        one.wait()


def per_device(inputs, out_grad, w_in, w_out, in_keep, out_keep):
    arrays = [
        pltpu.with_memory_space_constraint(array, pltpu.HBM)
        for array in (
            inputs.reshape(2, 4, 4, TOK // 8, BLOCK),
            out_grad.reshape(2, 4, 4, TOK // 8, BLOCK),
            w_in,
            w_out,
            in_keep,
            out_keep.reshape(1, -1),
        )
    ]
    vmem = pl.BlockSpec(memory_space=pltpu.VMEM)
    hbm = pl.BlockSpec(memory_space=pltpu.HBM)
    B, H, V = BLOCK, HID, pltpu.VMEM
    results = pl.pallas_call(
        kernel,
        out_shape=(
            jax.ShapeDtypeStruct((B, 2 * H), F32),
            jax.ShapeDtypeStruct((2 * H, B), F32),
            jax.ShapeDtypeStruct((ROWS, B), F32),
        ),
        in_specs=[hbm] * 6,
        out_specs=[vmem, vmem, vmem],
        scratch_shapes=[
            V((2, 4, 8, TOK // 8, 2 * B), BF),
            V((4, 2 * B, H), BF),
            V((4, H, 2 * B), BF),
            V((B, 2 * H), BF),
            V((2 * H, B), BF),
            V((B, H), BF),
            V((H, B), BF),
            pltpu.SMEM((1, 4), jnp.int32),
            pltpu.SMEM((1, 4), jnp.int32),
            V((2 * B, TOK), BF),
            V((TOK, H), F32),
            V((TOK, H), F32),
            V((4, 2 * B, H), BF),
            V((4, H, 2 * B), BF),
            V((2 * B, H), BF),
            V((H, 2 * B), BF),
            V((2 * B, H), BF),
            V((H, 2 * B), BF),
            V((2 * B, H), BF),
            V((H, 2 * B), BF),
            V((2 * B, H), F32),
            V((H, 2 * B), F32),
            V((2, B, H), BF),
            V((2, H, B), BF),
            V((2, 2, TOK, B), BF),
            V((2, 2, TOK, B), BF),
            V((2, 2, TOK, B), BF),
            V((2, 2, TOK, B), BF),
            V((8, HALF, B), BF),
            V((16, 16, B), BF),
            V((16, 16, B), BF),
            pltpu.SemaphoreType.DMA((N_SEM,)),
            pltpu.SemaphoreType.DMA((N_SEM,)),
            pltpu.SemaphoreType.DMA((6,)),
            pltpu.SemaphoreType.REGULAR((5,)),
        ],
        compiler_params=pltpu.CompilerParams(
            collective_id=0, has_side_effects=True, vmem_limit_bytes=48 * 1024 * 1024
        ),
    )(*arrays)
    return pl.pallas_call(
        write_out,
        out_shape=tuple(jax.ShapeDtypeStruct(r.shape, r.dtype) for r in results),
        in_specs=[vmem] * 3,
        out_specs=[hbm] * 3,
        scratch_shapes=[pltpu.SemaphoreType.DMA((3,))],
        compiler_params=pltpu.CompilerParams(vmem_limit_bytes=4 * 1024 * 1024),
    )(*results)


def solution(mesh):
    return jax.shard_map(
        per_device,
        mesh=mesh,
        in_specs=(
            P(None, "row"),
            P(None, "row"),
            P("row", "col"),
            P("col", "row"),
            P("row", "col"),
            P("col", "row"),
        ),
        out_specs=(P("row", "col"), P("col", "row"), P("col", "row")),
        check_vma=False,
    )
```

```python
import functools

import jax
import jax.numpy as jnp
from jax import lax
from jax.experimental import pallas as pl
from jax.experimental.pallas import tpu as pltpu
from jax.sharding import PartitionSpec as P

MESH = pl.DeviceIdType.MESH
BLOCK = 128
BF = jnp.bfloat16
F32 = jnp.float32

sqrt_two_pi = 0.7978845608028654
cubic_term = 0.044715

N_Y, N_XL, N_XH, N_Z = 4, 2, 2, 32
TOK = 384
HALF = 192
HID = 256
ROWS = 12


def tangent_of(value):
    return jnp.tanh(sqrt_two_pi * value * (1.0 + cubic_term * value * value))


def gelu(value):
    return 0.5 * value * (1.0 + tangent_of(value))


def gelu_slope(value):
    t = tangent_of(value)
    return 0.5 * (1.0 + t) + 0.5 * value * (1.0 - t * t) * sqrt_two_pi * (
        1.0 + 3.0 * cubic_term * value * value
    )


def nn(a, b):
    return jnp.dot(a, b, preferred_element_type=F32)


def nt(a, b):
    return lax.dot_general(a, b, (((1,), (1,)), ((), ())), preferred_element_type=F32)


class Names:
    def __init__(self):
        self.of = {}

    def __call__(self, *name):
        return self.of.setdefault(name, len(self.of))


N_SEM = 96


def kernel(
    inputs, out_grad, w_in, w_out, in_keep, out_keep,
    o_in, o_out, o_x,
    acts, win, wout, win_l, wout_l, win_s, wout_s, kin, kout, acts_t, pre, ag,
    v_in, v_out, ya_in, yb_out, y1_in, y1_out, y3_in, y3_out, s_in, s_out, x_in, x_out,
    q_o, q_m, q_r, q_s, z_r, f_s, f_r,
    send_sem, recv_sem, local_sem, relay_sem,
):
    row, col = lax.axis_index("row"), lax.axis_index("col")
    y, xl = row // N_XL, row % N_XL
    xh, z, k = col // (2 * N_Z), (col // 2) % N_Z, col % 2
    x = 2 * xh + xl
    h = z % 2
    pair = z + 1 - 2 * h

    def dev(y=y, x=x, z=z, k=k):
        return (y * N_XL + x % 2, ((x // 2) * N_Z + z) * 2 + k)

    def up(d):
        return (y + d) % N_Y

    def xr(d):
        return (x + d) % 4

    def along_z(d):
        return dev(z=(z + d + N_Z) % N_Z)

    core = dev(k=1 - k)
    inner = dev(x=2 * xh + 1 - xl)
    ydev = {d: dev(y=up(d)) for d in (1, 2, 3)}
    xdev = {d: dev(x=xr(d)) for d in (1, 3)}
    near = {
        (e, f): dev(x=xr(e), z=pair if f else z) for f in (0, 1) for e in range(4) if e or f
    }

    def owner(j):
        return dev(y=up(2 * h + k), z=8 * (j // 4) + 2 * y + j % 4 // 2, k=j % 2)

    barrier = pltpu.get_barrier_semaphore()
    partners = [core, *ydev.values(), *near.values(), along_z(2 * h - 1)]
    partners += [dev(y=up(d), k=1 - k) for d in (1, 2, 3)]
    for device in partners:
        pl.semaphore_signal(barrier, inc=1, device_id=device, device_id_type=MESH)

    names = Names()
    sent = []

    def copy(src, dst, name, device):
        i = names(*name)
        return pltpu.make_async_remote_copy(
            src_ref=src, dst_ref=dst, send_sem=send_sem.at[i], recv_sem=recv_sem.at[i],
            device_id=device, device_id_type=MESH,
        )

    def send(src, dst, name, device):
        c = copy(src, dst, name, device)
        c.start()
        sent.append(c)

    def arrived(dst, name):
        copy(dst, dst, name, core).wait_recv()

    def tell(r):
        for d in (-(1, 1, 2, 4, 8)[r], (1, 1, 2, 4, 8)[r]):
            pl.semaphore_signal(
                relay_sem.at[r], inc=1, device_id=along_z(d), device_id_type=MESH
            )

    def heard(r):
        pl.semaphore_wait(relay_sem.at[r], 2)

    local = [
        pltpu.make_async_copy(src, dst, local_sem.at[i])
        for i, (src, dst) in enumerate(
            ((w_in, win_l), (w_out, wout_l), (in_keep, kin), (out_keep, kout))
        )
    ]
    for c in local:
        c.start()
    for c in local:
        c.wait()

    def pruned_in(j):
        at = pl.ds(pl.multiple_of(j * BLOCK, BLOCK), BLOCK)
        return (win_l[:, at].astype(F32) * kin[0, j].astype(F32)).astype(BF)

    def pruned_out(j):
        at = pl.ds(pl.multiple_of(j * BLOCK, BLOCK), BLOCK)
        return (wout_l[at, :].astype(F32) * kout[0, j].astype(F32)).astype(BF)

    for jj in range(2):
        part = pl.ds(BLOCK * jj, BLOCK)
        win_s[:, part] = pruned_in(2 * (1 - xl) + jj)
        wout_s[part, :] = pruned_out(2 * (1 - xl) + jj)
        win[0, 0:BLOCK, part] = pruned_in(2 * xl + jj)
        wout[0, part, 0:BLOCK] = pruned_out(2 * xl + jj)

    pl.semaphore_wait(barrier, len(partners))

    def runs(half):
        return pl.ds(4 * half, 4)

    mine, other = runs(xh), runs(1 - xh)

    def tokens(array, of_y, half):
        return array.at[half, :, of_y]

    lo, hi = pl.ds(0, BLOCK), pl.ds(BLOCK, BLOCK)

    def win_at(d, p):
        return win.at[d, pl.ds(BLOCK * p, BLOCK), :]

    def wout_at(d, p):
        return wout.at[d, :, pl.ds(BLOCK * p, BLOCK)]

    def own_tokens(array):
        return [
            pltpu.make_async_copy(
                tokens(array, y, half), acts.at[k, 0, runs(half), :, lo], local_sem.at[4 + half]
            )
            for half in (0, 1)
        ]

    def first_copies(array):
        along_y = [
            copy(
                tokens(array, up(d), xh), acts.at[k, 4 - d, mine, :, lo], ("ay", 4 - d), ydev[d]
            )
            for d in (2, 1, 3)
        ]
        along_x = [
            copy(tokens(array, y, xh), acts.at[k, 0, mine, :, hi], ("ax", 0, 4 - d), xdev[d])
            for d in (1, 3)
        ]
        return along_y + along_x

    send(win_s, win_at(0, 1), ("wx_in",), inner)
    send(wout_s, wout_at(0, 1), ("wx_out",), inner)

    for i, array in enumerate((inputs, out_grad)):

        @pl.when(k == i)
        def _():
            for c in first_copies(array) + own_tokens(array):
                c.start()

    sent += first_copies(inputs)

    def spread(p):
        for d in (1, 3):
            send(win_at(0, p), win_at(4 - d, p), ("wy_in", 4 - d, p), ydev[d])
            send(wout_at(0, p), wout_at(4 - d, p), ("wy_out", 4 - d, p), ydev[d])

    spread(0)
    tell(0)

    def pass_on(p):
        arrived(win_at(3, p), ("wy_in", 3, p))
        send(win_at(3, p), win_at(2, p), ("wf_in", p), ydev[1])
        arrived(wout_at(1, p), ("wy_out", 1, p))
        send(wout_at(1, p), wout_at(2, p), ("wf_out", p), ydev[3])

    def token_half(e):
        return runs(xr(e) // 2)

    def from_x(d, e):
        return acts.at[k, d, token_half(e), :, hi]

    def both_x(d):
        for e in (1, 3):
            arrived(from_x(d, e), ("ax", d, e))
        if d == 2:
            away = 1 + 2 * k
            half = runs(((x + 4 - away) % 4) // 2)
            send(
                acts.at[k, d, half, :, hi],
                acts.at[k, d, half, :, lo],
                ("af", d),
                dev(x=(x + away) % 4),
            )
        elif d:
            send(from_x(d, d), acts.at[k, d, token_half(d), :, lo], ("af", d), xdev[4 - d])

    def to_core(d):
        if d:
            arrived(acts.at[k, d, other, :, lo], ("af", d))
        send(acts.at[k, d], acts.at[k, d], ("ac", d), core)

    def flat(i, d):
        return acts[i, d].reshape(TOK, 2 * BLOCK)

    def products(d):
        for p in (0, 1):
            if d == 1:
                arrived(win_at(1, p), ("wy_in", 1, p))
            if d == 3:
                arrived(wout_at(3, p), ("wy_out", 3, p))
            if d == 2:
                arrived(win_at(2, p), ("wf_in", p))
                arrived(wout_at(2, p), ("wf_out", p))
        arrived(acts.at[1 - k, d], ("ac", d))
        a, b = nn(flat(0, d), win[d]), nt(flat(1, d), wout[d])
        if d == 0:
            pre[...], ag[...] = a, b
        else:
            pre[...] += a
            ag[...] += b

    for d in (3, 1, 2):
        here = acts.at[k, d, mine, :, lo]
        arrived(here, ("ay", d))
        for e in (1, 3):
            send(here, acts.at[k, d, mine, :, hi], ("ax", d, 4 - e), xdev[e])
        if d == 3:
            heard(0)
            tell(1)

    arrived(win_at(0, 1), ("wx_in",))
    arrived(wout_at(0, 1), ("wx_out",))
    spread(1)
    heard(1)
    tell(2)
    pass_on(0)
    for c in own_tokens(inputs):
        c.wait()
    both_x(0)
    to_core(0)
    both_x(3)
    heard(2)
    tell(3)
    both_x(1)
    pass_on(1)
    products(0)
    both_x(2)
    for d in (3, 1, 2):
        to_core(d)
    products(3)
    heard(3)
    tell(4)
    products(1)
    products(2)

    pg = (ag[...] * gelu_slope(pre[...])).astype(BF)

    def slices(buffer, to_h, d):
        q = nt(pg, win[d]).astype(BF)
        buffer[to_h, 0] = q[:, 0:BLOCK]
        buffer[to_h, 1] = q[:, BLOCK:]

    def parity(f):
        return (h + f) % 2

    for f in (1, 0):
        slices(q_o, parity(f), 2 * parity(f) + 1 - k)
        send(q_o.at[parity(f)], q_r.at[parity(f)], ("q", f), core)
    for f in (1, 0):
        slices(q_m, parity(f), 2 * parity(f) + k)

    def rows_of(e):
        return pl.ds(pl.multiple_of(HALF * (xr(e) // 2), HALF), HALF)

    for f in (1, 0):
        to_h = parity(f)
        arrived(q_r.at[to_h], ("q", f))
        q_s[to_h] = (q_m[to_h].astype(F32) + q_r[to_h].astype(F32)).astype(BF)
        for e in (2, 1, 3, 0):
            if e or f:
                send(
                    q_s.at[to_h, e % 2, rows_of(e)],
                    z_r.at[4 * f + (4 - e) % 4],
                    ("z", (4 - e) % 4, f),
                    near[e, f],
                )
    total = q_s[h, 0, rows_of(0)].astype(F32)
    for e, f in ((0, 1), (1, 1), (3, 1), (1, 0), (3, 0), (2, 1), (2, 0)):
        arrived(z_r.at[4 * f + e], ("z", e, f))
        total += z_r[4 * f + e].astype(F32)

    f_s[...] = jnp.zeros_like(f_s)
    for j in range(16):
        f_s[j, 0:ROWS] = total[ROWS * j : ROWS * (j + 1)].astype(BF)
    heard(4)
    group = z // 2
    first = [names("f", g) for g in range(16)][0]
    own_owner = (h == 0) & (k == 0) & (z % 8 == 2 * y)

    def unless(own, act):
        if own is None:
            act()
        else:
            pl.when(jnp.logical_not(own))(act)

    far = []
    for j in range(16):
        own = own_owner & (z // 8 == j // 4) if j % 4 == 0 else None
        c = pltpu.make_async_remote_copy(
            src_ref=f_s.at[j], dst_ref=f_r.at[group], send_sem=send_sem.at[first + j],
            recv_sem=recv_sem.at[first + group], device_id=owner(j), device_id_type=MESH,
        )
        unless(own, c.start)
        far.append((own, c.wait_send))
        if own is not None:

            @pl.when(own)
            def _():
                f_r[group] = f_s[j]

    act_t = gelu(pre[...]).astype(BF).T

    def grads(d):
        acts_t[...] = flat(0, d).T
        v_in[d] = nn(acts_t[...], pg).astype(BF)
        v_out[d] = nn(act_t, flat(1, d)).astype(BF)

    grads(2)
    send(v_in.at[2], ya_in, ("ya",), ydev[1])
    send(v_out.at[2], yb_out, ("yb",), ydev[3])
    grads(1)
    send(v_out.at[1], y1_out, ("y1_out",), ydev[1])
    grads(3)
    send(v_in.at[3], y3_in, ("y3_in",), ydev[3])
    grads(0)

    arrived(ya_in, ("ya",))
    v_in[1] = (v_in[1].astype(F32) + ya_in[...].astype(F32)).astype(BF)
    send(v_in.at[1], y1_in, ("y1_in",), ydev[1])
    arrived(yb_out, ("yb",))
    v_out[3] = (v_out[3].astype(F32) + yb_out[...].astype(F32)).astype(BF)
    send(v_out.at[3], y3_out, ("y3_out",), ydev[3])

    arrived(y1_in, ("y1_in",))
    arrived(y3_in, ("y3_in",))
    s_in[...] = v_in[0].astype(F32) + y1_in[...].astype(F32) + y3_in[...].astype(F32)
    x_in[0] = s_in[BLOCK:].astype(BF)
    send(x_in.at[0], x_in.at[1], ("gx_in",), inner)
    arrived(y1_out, ("y1_out",))
    arrived(y3_out, ("y3_out",))
    s_out[...] = v_out[0].astype(F32) + y1_out[...].astype(F32) + y3_out[...].astype(F32)
    x_out[0] = s_out[:, BLOCK:].astype(BF)
    send(x_out.at[0], x_out.at[1], ("gx_out",), inner)

    def store_in(j, value):
        at = pl.ds(pl.multiple_of(j * BLOCK, BLOCK), BLOCK)
        o_in[:, at] = value * kin[0, j].astype(F32)

    def store_out(j, value):
        at = pl.ds(pl.multiple_of(j * BLOCK, BLOCK), BLOCK)
        o_out[at, :] = value * kout[0, j].astype(F32)

    cuts = [pl.ds(BLOCK * jj, BLOCK) for jj in (0, 1)]
    for jj, cut in enumerate(cuts):
        store_in(2 * xl + jj, s_in[0:BLOCK, cut])
        store_out(2 * xl + jj, s_out[cut, 0:BLOCK])
    arrived(x_in.at[1], ("gx_in",))
    for jj, cut in enumerate(cuts):
        store_in(2 * (1 - xl) + jj, x_in[1, :, cut].astype(F32))
    arrived(x_out.at[1], ("gx_out",))
    for jj, cut in enumerate(cuts):
        store_out(2 * (1 - xl) + jj, x_out[1, cut, :].astype(F32))

    for c in sent:
        c.wait_send()
    for own, wait in far:
        unless(own, wait)

    for g in range(16):
        unless(own_owner & (group == g), functools.partial(arrived, f_r.at[g], ("f", g)))
    last = f_r[0].astype(F32)
    for g in range(1, 16):
        last += f_r[g].astype(F32)
    o_x[...] = last[0:ROWS]


def write_out(a, b, c, a_out, b_out, c_out, sem):
    pairs = ((a, a_out), (b, b_out), (c, c_out))
    copies = [pltpu.make_async_copy(src, dst, sem.at[i]) for i, (src, dst) in enumerate(pairs)]
    for one in copies:
        one.start()
    for one in copies:
        one.wait()


def per_device(inputs, out_grad, w_in, w_out, in_keep, out_keep):
    arrays = [
        pltpu.with_memory_space_constraint(array, pltpu.HBM)
        for array in (
            inputs.reshape(2, 4, 4, TOK // 8, BLOCK),
            out_grad.reshape(2, 4, 4, TOK // 8, BLOCK),
            w_in,
            w_out,
            in_keep,
            out_keep.reshape(1, -1),
        )
    ]
    vmem = pl.BlockSpec(memory_space=pltpu.VMEM)
    hbm = pl.BlockSpec(memory_space=pltpu.HBM)
    B, H, V = BLOCK, HID, pltpu.VMEM
    results = pl.pallas_call(
        kernel,
        out_shape=(
            jax.ShapeDtypeStruct((B, 2 * H), F32),
            jax.ShapeDtypeStruct((2 * H, B), F32),
            jax.ShapeDtypeStruct((ROWS, B), F32),
        ),
        in_specs=[hbm] * 6,
        out_specs=[vmem, vmem, vmem],
        scratch_shapes=[
            V((2, 4, 8, TOK // 8, 2 * B), BF),
            V((4, 2 * B, H), BF),
            V((4, H, 2 * B), BF),
            V((B, 2 * H), BF),
            V((2 * H, B), BF),
            V((B, H), BF),
            V((H, B), BF),
            pltpu.SMEM((1, 4), jnp.int32),
            pltpu.SMEM((1, 4), jnp.int32),
            V((2 * B, TOK), BF),
            V((TOK, H), F32),
            V((TOK, H), F32),
            V((4, 2 * B, H), BF),
            V((4, H, 2 * B), BF),
            V((2 * B, H), BF),
            V((H, 2 * B), BF),
            V((2 * B, H), BF),
            V((H, 2 * B), BF),
            V((2 * B, H), BF),
            V((H, 2 * B), BF),
            V((2 * B, H), F32),
            V((H, 2 * B), F32),
            V((2, B, H), BF),
            V((2, H, B), BF),
            V((2, 2, TOK, B), BF),
            V((2, 2, TOK, B), BF),
            V((2, 2, TOK, B), BF),
            V((2, 2, TOK, B), BF),
            V((8, HALF, B), BF),
            V((16, 16, B), BF),
            V((16, 16, B), BF),
            pltpu.SemaphoreType.DMA((N_SEM,)),
            pltpu.SemaphoreType.DMA((N_SEM,)),
            pltpu.SemaphoreType.DMA((6,)),
            pltpu.SemaphoreType.REGULAR((5,)),
        ],
        compiler_params=pltpu.CompilerParams(
            collective_id=0, has_side_effects=True, vmem_limit_bytes=48 * 1024 * 1024
        ),
    )(*arrays)
    return pl.pallas_call(
        write_out,
        out_shape=tuple(jax.ShapeDtypeStruct(r.shape, r.dtype) for r in results),
        in_specs=[vmem] * 3,
        out_specs=[hbm] * 3,
        scratch_shapes=[pltpu.SemaphoreType.DMA((3,))],
        compiler_params=pltpu.CompilerParams(vmem_limit_bytes=4 * 1024 * 1024),
    )(*results)


def solution(mesh):
    return jax.shard_map(
        per_device,
        mesh=mesh,
        in_specs=(
            P(None, "row"),
            P(None, "row"),
            P("row", "col"),
            P("col", "row"),
            P("row", "col"),
            P("col", "row"),
        ),
        out_specs=(P("row", "col"), P("col", "row"), P("col", "row")),
        check_vma=False,
    )
```
